1024 devices in a mesh: wide: 32 (over z_lo, core), narrow: 32 (over y, x, z_hi).
Axes of the slice: x: 4, y: 4, z: 32 (z_hi: 2, z_lo: 16; z = z_hi * 16 + z_lo), core: 2. Of those that a mesh axis runs over, the one named last changes fastest.
Arguments:
- left_values: bfloat16 [32, 64, 128, 128], P('wide', 'narrow'), may hold values from -6 to 6
- right_values: bfloat16 [64, 32, 128, 128], P('wide', 'narrow'), may hold values from -0.25 to 0.25
- stack_left: int32 [32, 32, 64, 4], P('wide', 'narrow'), may hold values from 0 to 63
- stack_right: int32 [32, 32, 64, 4], P('wide', 'narrow'), may hold values from 0 to 63
- stack_slot: int32 [32, 32, 64], P('wide', 'narrow'), may hold values from 0 to 7
- stack_count: int32 [32, 32], P('wide', 'narrow'), may hold values from 1 to 64, as said below
Outputs:
- product: float32 [32, 256, 128, 128], P('wide', 'narrow')
The draws below stay inside these ranges and needn't reach their ends.
Inputs may be any that keep to these rules, and one draw needn't show every extreme that they name: Stacks at positions stack_count[w, n] and beyond are unused; some entry equals 64.
All inputs are finite; a program needn't handle non-finite values.
Results may differ from the reference program's by a relative error of at most 0.0003.
Values may be sent and summed in bfloat16 or wider, within the bound.
No kernel may reach another device: no remote copies, remote signals or barrier semaphores. Data moves between devices by JAX's collectives and lax.ppermute only.
A program may use at most 32 MiB of HBM per device.

```python
import jax
import jax.numpy as jnp
from jax import lax

BS = 128
STACKS = 64
STACK = 4
CSLOT = 8
ABLOCKS = 64
BBLOCKS = 64
N_WIDE = 32
N_NARROW = 32


def draw_stack_count(key, part):
    key = jax.random.fold_in(key, 11)
    first, second, third = jax.random.split(key, 3)
    shape = (N_WIDE, N_NARROW)
    level = jax.random.randint(first, shape, 0, 4)
    top = jnp.right_shift(jnp.full(shape, STACKS, jnp.int32), level.astype(jnp.int32))
    jitter = jax.random.randint(second, shape, 0, 1 + jnp.right_shift(top, 1))
    counts = top - jitter
    chosen = jax.random.randint(third, (), 0, N_WIDE * N_NARROW)
    places = jnp.arange(N_WIDE * N_NARROW, dtype=jnp.int32).reshape(shape)
    return jnp.where(places == chosen, STACKS, counts).astype(jnp.int32)


def set_ends(values, key, low, largest):
    extent = values.shape
    spot = [jax.random.randint(jax.random.fold_in(key, axis), (), 0, extent[axis]) for axis in range(len(extent))]
    values = values.at[tuple(spot)].set(low)
    longest = extent.index(max(extent))
    spot[longest] = (spot[longest] + 1) % extent[longest]
    return values.at[tuple(spot)].set(largest)


def shard_levels(rng, dims, shards, low, largest):
    def one(axis_at, shards_of):
        heights = jax.random.uniform(jax.random.fold_in(jax.random.fold_in(rng, 6), axis_at), (shards_of,), jnp.float32, low / len(shards), largest / len(shards))
        return jnp.repeat(jnp.exp(heights), dims[axis_at] // shards_of).reshape((-1,) + (1,) * (len(dims) - axis_at - 1))

    loudness = one(*shards[0])
    for cut in shards[1:]:
        loudness = loudness * one(*cut)
    return loudness


def noise(stream_key, shape, spread, reach, cuts=(), held_as=jnp.bfloat16):
    array = jax.random.normal(stream_key, shape, jnp.float32) * spread
    if len(cuts) > 0:
        array = shard_levels(stream_key, shape, cuts, -0.22, 0.18) * array
    return jnp.clip(array, min=-reach, max=reach).astype(held_as)


def setup_inputs(seed: int = 0) -> dict:
    key_of = jax.random.split(jax.random.key(seed), 7)
    left_values = noise(key_of[0], (N_WIDE, ABLOCKS, BS, BS), 1.0, 6.0, ((0, 32), (1, 32)))
    right_values = noise(key_of[1], (BBLOCKS, N_NARROW, BS, BS), (BS * STACK) ** -0.5, 0.25, ((0, 32), (1, 32)))
    stack_left = set_ends(jax.random.randint(key_of[2], (N_WIDE, N_NARROW, STACKS, STACK), 0, ABLOCKS), jax.random.fold_in(key_of[2], 1), 0, ABLOCKS - 1).astype(jnp.int32)
    stack_right = set_ends(jax.random.randint(key_of[3], (N_WIDE, N_NARROW, STACKS, STACK), 0, BBLOCKS), jax.random.fold_in(key_of[3], 1), 0, BBLOCKS - 1).astype(jnp.int32)
    stack_slot = set_ends(jax.random.randint(key_of[4], (N_WIDE, N_NARROW, STACKS), 0, CSLOT), jax.random.fold_in(key_of[4], 1), 0, CSLOT - 1).astype(jnp.int32)
    stack_count = draw_stack_count(jax.random.fold_in(key_of[6], 71), 0)
    return {"left_values": left_values, "right_values": right_values, "stack_left": stack_left, "stack_right": stack_right, "stack_slot": stack_slot, "stack_count": stack_count}


def stack_terms(total, left_rows, right_cols, lefts, rights, slots, count):
    group = min(16, STACKS)

    def step(index, acc):
        start = index * group
        pick_a = lax.dynamic_slice_in_dim(lefts, start, group, 0)
        pick_b = lax.dynamic_slice_in_dim(rights, start, group, 0)
        pick_c = lax.dynamic_slice_in_dim(slots, start, group, 0)
        chosen_a = left_rows[pick_a].astype(jnp.float32)
        chosen_b = right_cols[pick_b].astype(jnp.float32)
        sums = jnp.einsum('gsij,gsjk->gik', chosen_a, chosen_b)
        places = start + jnp.arange(group, dtype=jnp.int32)
        live = places < count
        match = (pick_c[None, :] == jnp.arange(CSLOT, dtype=jnp.int32)[:, None]) & live[None, :]
        onehot = jnp.where(match, 1.0, 0.0).astype(jnp.float32)
        return acc + jnp.einsum('cg,gij->cij', onehot, sums, precision=lax.Precision.HIGHEST)

    upper = ((count + group - 1) // group).astype(jnp.int32)
    return lax.fori_loop(jnp.int32(0), upper, step, total)


def reference(left_values, right_values, stack_left, stack_right, stack_slot, stack_count):
    def one_row(row):
        left_rows = left_values[row]

        def one_column(col):
            right_cols = right_values[:, col]
            empty = jnp.zeros((CSLOT, BS, BS), jnp.float32)
            return stack_terms(empty, left_rows, right_cols, stack_left[row, col], stack_right[row, col], stack_slot[row, col], stack_count[row, col])

        return lax.map(one_column, jnp.arange(N_NARROW, dtype=jnp.int32))

    whole = lax.map(one_row, jnp.arange(N_WIDE, dtype=jnp.int32))
    return whole.reshape(N_WIDE, N_NARROW * CSLOT, BS, BS)
```

```python
import jax
import jax.numpy as jnp
from jax import lax
from jax.experimental import pallas as pl
from jax.experimental.pallas import tpu as pltpu
from jax.sharding import Mesh
from jax.sharding import PartitionSpec as P

CSLOT = 8
UNROLL = 8
Z_HI, Z_LO = 4, 4
AXES = ("za", "zb", "core", "y", "x", "zh")
SIZES = (Z_HI, Z_LO, 2, 4, 4, 2)


def swap(value, axis, size, bits):
    return lax.ppermute(value, axis, [(i, i ^ bits) for i in range(size)])


def gather_plane(value):
    spread = jnp.broadcast_to(value[None], (16,) + value.shape)
    return lax.all_to_all(spread, ("y", "x"), split_axis=0, concat_axis=0, tiled=True)


def stacks_kernel(meta, own_h, far_h, a_h, b_h, ca_h, cb_h, out, left, right, sems):
    copies = [
        pltpu.make_async_copy(src, dst, sems.at[i])
        for i, (src, dst) in enumerate(
            (
                (own_h, left.at[pl.ds(0, 32)]),
                (far_h, left.at[pl.ds(32, 32)]),
                (a_h, right.at[pl.ds(0, 8)]),
                (b_h, right.at[pl.ds(8, 24)]),
                (ca_h, right.at[pl.ds(32, 8)]),
                (cb_h, right.at[pl.ds(40, 24)]),
            )
        )
    ]
    for copy in copies:
        copy.start()
    out[...] = jnp.zeros_like(out)
    za, zb, core, half = meta[577], meta[578], meta[579], meta[580]
    count = meta[576]

    def left_at(slot):
        place = ((slot >> 2) << 1) + (slot & 1)
        return place + ((((slot >> 1) & 1) ^ half) << 5)

    def right_at(slot):
        far = (slot >> 4) ^ za
        far = ((far & 1) << 1) + (far >> 1)
        near = ((slot >> 2) & 3) ^ zb
        other = ((slot >> 1) & 1) ^ core
        return (other << 5) + (near << 3) + (far << 1) + (slot & 1)

    def stack_sum(t):
        lefts = [left[left_at(meta[4 * t + g])] for g in range(4)]
        rights = [right[right_at(meta[256 + 4 * t + g])] for g in range(4)]
        return jnp.dot(
            jnp.concatenate(lefts, 1),
            jnp.concatenate(rights, 0),
            preferred_element_type=jnp.float32,
        )

    for copy in copies:
        copy.wait()

    def add(first, width):
        sums = [stack_sum(first + u) for u in range(width)]
        for u in range(width):
            slot = meta[512 + first + u]
            out[slot] = out[slot] + sums[u]

    def wide_step(i, carry):
        add(i * UNROLL, UNROLL)
        return carry

    def single_step(t, carry):
        add(t, 1)
        return carry

    groups = count // UNROLL
    lax.fori_loop(0, groups, wide_step, 0)
    lax.fori_loop(groups * UNROLL, count, single_step, 0)


def body(left_values, right_values, stack_left, stack_right, stack_slot, stack_count):
    own_left = left_values[0]
    own_right = right_values[:, 0]
    places = [lax.axis_index(a) for a in ("za", "zb", "core", "zh")]
    meta = jnp.concatenate(
        [
            stack_left.reshape(-1),
            stack_right.reshape(-1),
            stack_slot.reshape(-1),
            stack_count.reshape(-1),
            jnp.stack(places).astype(jnp.int32),
        ]
    )
    right_8 = swap(own_right, "za", Z_HI, 2)
    far_left = swap(own_left, "zh", 2, 1)
    pair = jnp.concatenate([own_right, right_8], 0)
    right_4 = swap(pair, "za", Z_HI, 1)
    plane_own = gather_plane(own_left)
    a = jnp.concatenate([pair, right_4], 0)
    b = jnp.concatenate([swap(a, "zb", Z_LO, k) for k in (1, 2, 3)], 0)
    plane_far = gather_plane(far_left)
    ca = swap(a, "core", 2, 1)
    cb = swap(b, "core", 2, 1)
    block = own_left.shape[1]
    return pl.pallas_call(
        stacks_kernel,
        out_shape=jax.ShapeDtypeStruct((CSLOT, block, block), jnp.float32),
        in_specs=[pl.BlockSpec(memory_space=pltpu.SMEM)]
        + [pl.BlockSpec(memory_space=pl.ANY)] * 6,
        out_specs=pl.BlockSpec(memory_space=pltpu.VMEM),
        scratch_shapes=[
            pltpu.VMEM((64, block, block), jnp.bfloat16),
            pltpu.VMEM((64, block, block), jnp.bfloat16),
            pltpu.SemaphoreType.DMA((6,)),
        ],
        compiler_params=pltpu.CompilerParams(vmem_limit_bytes=16 << 20),
    )(meta, plane_own.reshape(32, block, block), plane_far.reshape(32, block, block), a, b, ca, cb)[None]


def solution(mesh):
    fine = Mesh(mesh.devices.reshape(SIZES), AXES)
    wide, narrow = ("za", "zb", "core"), ("y", "x", "zh")
    return jax.shard_map(
        body,
        mesh=fine,
        in_specs=(
            P(wide, narrow, None, None),
            P(wide, narrow, None, None),
            P(wide, narrow, None, None),
            P(wide, narrow, None, None),
            P(wide, narrow, None),
            P(wide, narrow),
        ),
        out_specs=P(wide, narrow, None, None),
        check_vma=False,
    )
```

```python
import jax
import jax.numpy as jnp
from jax import lax
from jax.experimental import pallas as pl
from jax.experimental.pallas import tpu as pltpu
from jax.sharding import Mesh
from jax.sharding import PartitionSpec as P

CSLOT = 8
UNROLL = 8
Z_HI, Z_LO = 4, 4
AXES = ("za", "zb", "core", "y", "x", "zh")
SIZES = (Z_HI, Z_LO, 2, 4, 4, 2)


def swap(value, axis, size, bits):
    return lax.ppermute(value, axis, [(i, i ^ bits) for i in range(size)])


def gather_plane(value):
    spread = jnp.broadcast_to(value[None], (16,) + value.shape)
    return lax.all_to_all(spread, ("y", "x"), split_axis=0, concat_axis=0, tiled=True)


def stacks_kernel(meta, left_h, *refs):
    pieces, (out, left, right, sems) = refs[:8], refs[8:]
    copies = [pltpu.make_async_copy(left_h, left, sems.at[8])]
    copies += [
        pltpu.make_async_copy(piece, right.at[pl.ds(8 * i, 8)], sems.at[i])
        for i, piece in enumerate(pieces)
    ]
    for copy in copies:
        copy.start()
    out[...] = jnp.zeros_like(out)
    za, zb, core, half = meta[577], meta[578], meta[579], meta[580]
    count = meta[576]

    def left_at(slot):
        return slot ^ (half << 1)

    def right_at(slot):
        far = (slot >> 4) ^ za
        far = ((far & 1) << 1) + (far >> 1)
        near = ((slot >> 2) & 3) ^ zb
        other = ((slot >> 1) & 1) ^ core
        return (other << 5) + (near << 3) + (far << 1) + (slot & 1)

    def stack_sum(t):
        lefts = [left[left_at(meta[4 * t + g])] for g in range(4)]
        rights = [right[right_at(meta[256 + 4 * t + g])] for g in range(4)]
        return jnp.dot(
            jnp.concatenate(lefts, 1),
            jnp.concatenate(rights, 0),
            preferred_element_type=jnp.float32,
        )

    for copy in copies:
        copy.wait()

    def add(first, width):
        sums = [stack_sum(first + u) for u in range(width)]
        for u in range(width):
            slot = meta[512 + first + u]
            out[slot] = out[slot] + sums[u]

    def wide_step(i, carry):
        add(i * UNROLL, UNROLL)
        return carry

    def single_step(t, carry):
        add(t, 1)
        return carry

    groups = count // UNROLL
    lax.fori_loop(0, groups, wide_step, 0)
    lax.fori_loop(groups * UNROLL, count, single_step, 0)


def body(left_values, right_values, stack_left, stack_right, stack_slot, stack_count):
    own_left = left_values[0]
    own_right = right_values[:, 0]
    places = [lax.axis_index(a) for a in ("za", "zb", "core", "zh")]
    meta = jnp.concatenate(
        [
            stack_left.reshape(-1),
            stack_right.reshape(-1),
            stack_slot.reshape(-1),
            stack_count.reshape(-1),
            jnp.stack(places).astype(jnp.int32),
        ]
    )
    right_8 = swap(own_right, "za", Z_HI, 2)
    far_left = swap(own_left, "zh", 2, 1)
    right_8, far_left = lax.optimization_barrier((right_8, far_left))
    pair = jnp.concatenate([own_right, right_8], 0)
    right_4 = swap(pair, "za", Z_HI, 1)
    plane = gather_plane(jnp.concatenate([own_left, far_left], 0))
    a = jnp.concatenate([pair, right_4], 0)
    near = [a] + [swap(a, "zb", Z_LO, k) for k in (1, 2, 3)]
    pieces = near + [swap(piece, "core", 2, 1) for piece in near]
    block = own_left.shape[1]
    return pl.pallas_call(
        stacks_kernel,
        out_shape=jax.ShapeDtypeStruct((CSLOT, block, block), jnp.float32),
        in_specs=[pl.BlockSpec(memory_space=pltpu.SMEM)]
        + [pl.BlockSpec(memory_space=pl.ANY)] * 9,
        out_specs=pl.BlockSpec(memory_space=pltpu.VMEM),
        scratch_shapes=[
            pltpu.VMEM((64, block, block), jnp.bfloat16),
            pltpu.VMEM((64, block, block), jnp.bfloat16),
            pltpu.SemaphoreType.DMA((9,)),
        ],
        compiler_params=pltpu.CompilerParams(vmem_limit_bytes=16 << 20),
    )(meta, plane.reshape(64, block, block), *pieces)[None]


def solution(mesh):
    fine = Mesh(mesh.devices.reshape(SIZES), AXES)
    wide, narrow = ("za", "zb", "core"), ("y", "x", "zh")
    return jax.shard_map(
        body,
        mesh=fine,
        in_specs=(
            P(wide, narrow, None, None),
            P(wide, narrow, None, None),
            P(wide, narrow, None, None),
            P(wide, narrow, None, None),
            P(wide, narrow, None),
            P(wide, narrow),
        ),
        out_specs=P(wide, narrow, None, None),
        check_vma=False,
    )
```

```python
import jax
import jax.numpy as jnp
from jax import lax
from jax.experimental import pallas as pl
from jax.experimental.pallas import tpu as pltpu
from jax.sharding import Mesh
from jax.sharding import PartitionSpec as P

CSLOT = 8
UNROLL = 8
Z_HI, Z_LO = 4, 4
AXES = ("za", "zb", "core", "y", "x", "zh")
SIZES = (Z_HI, Z_LO, 2, 4, 4, 2)
LONG = 10**11


def swap(value, axis, size, bits):
    return lax.ppermute(value, axis, [(i, i ^ bits) for i in range(size)])


def gather_plane(value):
    spread = jnp.broadcast_to(value[None], (16,) + value.shape)
    return lax.all_to_all(spread, ("y", "x"), split_axis=0, concat_axis=0, tiled=True)


def hold(value, name):
    def kernel(ref, same):
        pass

    return pl.pallas_call(
        kernel,
        out_shape=jax.ShapeDtypeStruct(value.shape, value.dtype),
        in_specs=[pl.BlockSpec(memory_space=pl.ANY)],
        out_specs=pl.BlockSpec(memory_space=pl.ANY),
        input_output_aliases={0: 0},
        cost_estimate=pl.CostEstimate(flops=LONG, bytes_accessed=0, transcendentals=0),
        name=name,
    )(value)


def stacks_kernel(lefts_at, rights_at, slots, counts, left, *refs):
    pieces, (out, right) = refs[:-2], refs[-2:]
    first = 0
    for piece in pieces:
        right[pl.ds(first, piece.shape[0])] = piece[...]
        first += piece.shape[0]
    out[...] = jnp.zeros_like(out)
    za, zb, core, half = (lax.axis_index(a) for a in ("za", "zb", "core", "zh"))
    count = counts[0, 0]

    def left_at(slot):
        return slot ^ (half << 1)

    def right_at(slot):
        far = (slot >> 4) ^ za
        near = ((slot >> 2) & 3) ^ zb
        other = ((slot >> 1) & 1) ^ core
        return (other << 5) + ((far & 1) << 4) + (near << 2) + (far & 2) + (slot & 1)

    def stack_sum(t):
        lefts = [left[left_at(lefts_at[g, t])] for g in range(4)]
        rights = [right[right_at(rights_at[g, t])] for g in range(4)]
        return jnp.dot(
            jnp.concatenate(lefts, 1),
            jnp.concatenate(rights, 0),
            preferred_element_type=jnp.float32,
        )

    def step(i, carry):
        first = i * UNROLL
        sums = [stack_sum(first + u) for u in range(UNROLL)]
        for u in range(UNROLL):
            slot = slots[first + u]
            out[slot] = out[slot] + jnp.where(first + u < count, sums[u], 0.0)
        return carry

    lax.fori_loop(0, lax.div(count + UNROLL - 1, UNROLL), step, 0)


def body(left_values, right_values, stack_left, stack_right, stack_slot, stack_count):
    own_left = left_values[0]
    own_right = right_values[:, 0]
    right_8 = swap(own_right, "za", Z_HI, 2)
    far_left = swap(own_left, "zh", 2, 1)
    pair = hold(jnp.concatenate([own_right, right_8], 0), "pair")
    right_4 = swap(pair, "za", Z_HI, 1)
    early = [swap(pair, "zb", Z_LO, k) for k in (1, 2, 3)]
    rest = hold(right_4, "rest")
    plane = gather_plane(jnp.concatenate([own_left, far_left], 0))
    late = [swap(rest, "zb", Z_LO, k) for k in (1, 2, 3)]
    early = jnp.concatenate([pair] + early, 0)
    late = jnp.concatenate([rest] + late, 0)
    pieces = [early, late]
    pieces += [swap(piece, "core", 2, 1) for piece in pieces]
    block = own_left.shape[1]
    return pl.pallas_call(
        stacks_kernel,
        out_shape=jax.ShapeDtypeStruct((CSLOT, block, block), jnp.float32),
        in_specs=[pl.BlockSpec(memory_space=pltpu.SMEM)] * 4
        + [pl.BlockSpec(memory_space=pltpu.VMEM)] * (1 + len(pieces)),
        out_specs=pl.BlockSpec(memory_space=pltpu.VMEM),
        scratch_shapes=[pltpu.VMEM((64, block, block), jnp.bfloat16)],
        compiler_params=pltpu.CompilerParams(vmem_limit_bytes=32 << 20),
    )(
        stack_left[0, 0].T,
        stack_right[0, 0].T,
        stack_slot[0, 0],
        stack_count,
        plane.reshape(64, block, block),
        *pieces,
    )[None]


def solution(mesh):
    fine = Mesh(mesh.devices.reshape(SIZES), AXES)
    wide, narrow = ("za", "zb", "core"), ("y", "x", "zh")
    return jax.shard_map(
        body,
        mesh=fine,
        in_specs=(
            P(wide, narrow, None, None),
            P(wide, narrow, None, None),
            P(wide, narrow, None, None),
            P(wide, narrow, None, None),
            P(wide, narrow, None),
            P(wide, narrow),
        ),
        out_specs=P(wide, narrow, None, None),
        check_vma=False,
    )
```

```python
import jax
import jax.numpy as jnp
from jax import lax
from jax.experimental import pallas as pl
from jax.experimental.pallas import tpu as pltpu
from jax.sharding import Mesh
from jax.sharding import PartitionSpec as P

CSLOT = 8
UNROLL = 16
Z_HI, Z_LO = 4, 4
AXES = ("za", "zb", "core", "y", "x", "zh")
SIZES = (Z_HI, Z_LO, 2, 4, 4, 2)
LONG = 10**11


def swap(value, axis, size, bits):
    return lax.ppermute(value, axis, [(i, i ^ bits) for i in range(size)])


def exchange_plane(value):
    return lax.all_to_all(value, ("y", "x"), split_axis=0, concat_axis=0, tiled=True)


def hold(value, name, cost=0):
    def kernel(ref, same):
        pass

    return pl.pallas_call(
        kernel,
        out_shape=pltpu.VMEM(value.shape, value.dtype),
        in_specs=[pl.BlockSpec(memory_space=pltpu.VMEM)],
        out_specs=pl.BlockSpec(memory_space=pltpu.VMEM),
        input_output_aliases={0: 0},
        cost_estimate=pl.CostEstimate(flops=cost, bytes_accessed=0, transcendentals=0),
        name=name,
    )(value)


def stacks_kernel(lefts_at, rights_at, slots, counts, left, *refs):
    pieces, (out, right, sems) = refs[:-3], refs[-3:]
    own, other = pieces[: len(pieces) // 2], pieces[len(pieces) // 2 :]
    copies, first = [], 32
    for i, piece in enumerate(other):
        place = right.at[pl.ds(first, piece.shape[0])]
        copies.append(pltpu.make_async_copy(piece, place, sems.at[i]))
        copies[-1].start()
        first += piece.shape[0]
    first = 0
    for piece in own:
        right[pl.ds(first, piece.shape[0])] = piece[...]
        first += piece.shape[0]
    out[...] = jnp.zeros_like(out)
    za, zb, core, half = (lax.axis_index(a) for a in ("za", "zb", "core", "zh"))
    count = counts[0, 0]

    def left_at(slot):
        return slot ^ (half << 1)

    def right_at(slot):
        far = (slot >> 4) ^ za
        near = ((slot >> 2) & 3) ^ zb
        other = ((slot >> 1) & 1) ^ core
        return (other << 5) + ((far & 1) << 4) + (near << 2) + (far & 2) + (slot & 1)

    def stack_sum(t):
        lefts = [left[left_at(lefts_at[g, t])] for g in range(4)]
        rights = [right[right_at(rights_at[g, t])] for g in range(4)]
        return jnp.dot(
            jnp.concatenate(lefts, 1),
            jnp.concatenate(rights, 0),
            preferred_element_type=jnp.float32,
        )

    for copy in copies:
        copy.wait()

    def step(i, carry):
        first = i * UNROLL
        sums = [stack_sum(first + u) for u in range(UNROLL)]
        for u in range(UNROLL):
            slot = slots[first + u]
            out[slot] = out[slot] + jnp.where(first + u < count, sums[u], 0.0)
        return carry

    lax.fori_loop(0, lax.div(count + UNROLL - 1, UNROLL), step, 0)


def body(left_values, right_values, stack_left, stack_right, stack_slot, stack_count):
    own_left = left_values[0]
    own_right = right_values[:, 0]
    right_8 = swap(own_right, "za", Z_HI, 2)
    far_left = swap(own_left, "zh", 2, 1)
    pair = hold(jnp.concatenate([own_right, right_8], 0), "pair", LONG)
    right_4 = swap(pair, "za", Z_HI, 1)
    early = [swap(pair, "zb", Z_LO, k) for k in (1, 2, 3)]
    rest = hold(right_4, "rest", LONG)
    halves = jnp.concatenate([own_left, far_left], 0)
    plane = exchange_plane(jnp.broadcast_to(halves[None], (16,) + halves.shape))
    late = [swap(rest, "zb", Z_LO, k) for k in (1, 2, 3)]
    early = jnp.concatenate([pair] + early, 0)
    late = jnp.concatenate([rest] + late, 0)
    pieces = [early, late]
    pieces += [
        pltpu.with_memory_space_constraint(swap(piece, "core", 2, 1), pltpu.HBM)
        for piece in pieces
    ]
    block = own_left.shape[1]
    return pl.pallas_call(
        stacks_kernel,
        out_shape=jax.ShapeDtypeStruct((CSLOT, block, block), jnp.float32),
        in_specs=[pl.BlockSpec(memory_space=pltpu.SMEM)] * 4
        + [pl.BlockSpec(memory_space=pltpu.VMEM)] * (1 + len(pieces) // 2)
        + [pl.BlockSpec(memory_space=pltpu.HBM)] * (len(pieces) // 2),
        out_specs=pl.BlockSpec(memory_space=pltpu.VMEM),
        scratch_shapes=[
            pltpu.VMEM((64, block, block), jnp.bfloat16),
            pltpu.SemaphoreType.DMA((len(pieces) // 2,)),
        ],
        compiler_params=pltpu.CompilerParams(vmem_limit_bytes=8 << 20),
    )(
        stack_left[0, 0].T,
        stack_right[0, 0].T,
        stack_slot[0, 0],
        stack_count,
        plane.reshape(64, block, block),
        *pieces,
    )[None]


def solution(mesh):
    fine = Mesh(mesh.devices.reshape(SIZES), AXES)
    wide, narrow = ("za", "zb", "core"), ("y", "x", "zh")
    return jax.shard_map(
        body,
        mesh=fine,
        in_specs=(
            P(wide, narrow, None, None),
            P(wide, narrow, None, None),
            P(wide, narrow, None, None),
            P(wide, narrow, None, None),
            P(wide, narrow, None),
            P(wide, narrow),
        ),
        out_specs=P(wide, narrow, None, None),
        check_vma=False,
    )
```

```python
import jax
import jax.numpy as jnp
from jax import lax
from jax.experimental import pallas as pl
from jax.experimental.pallas import tpu as pltpu
from jax.sharding import Mesh
from jax.sharding import PartitionSpec as P

CSLOT = 8
UNROLL = 16
Z_HI, Z_LO = 4, 4
AXES = ("za", "zb", "core", "y", "x", "zh")
SIZES = (Z_HI, Z_LO, 2, 4, 4, 2)
LONG = 10**11


def swap(value, axis, size, bits):
    return lax.ppermute(value, axis, [(i, i ^ bits) for i in range(size)])


def exchange_plane(value):
    return lax.all_to_all(value, ("x", "y"), split_axis=0, concat_axis=0, tiled=True)


def hold(value, name, cost=0):
    def kernel(ref, same):
        pass

    return pl.pallas_call(
        kernel,
        out_shape=pltpu.VMEM(value.shape, value.dtype),
        in_specs=[pl.BlockSpec(memory_space=pltpu.VMEM)],
        out_specs=pl.BlockSpec(memory_space=pltpu.VMEM),
        input_output_aliases={0: 0},
        cost_estimate=pl.CostEstimate(flops=cost, bytes_accessed=0, transcendentals=0),
        name=name,
    )(value)


def stacks_kernel(lefts_at, rights_at, slots, counts, left, *refs):
    pieces, (out, right, sems) = refs[:-3], refs[-3:]
    own, other = pieces[: len(pieces) // 2], pieces[len(pieces) // 2 :]
    copies, first = [], 32
    for i, piece in enumerate(other):
        place = right.at[pl.ds(first, piece.shape[0])]
        copies.append(pltpu.make_async_copy(piece, place, sems.at[i]))
        copies[-1].start()
        first += piece.shape[0]
    first = 0
    for piece in own:
        right[pl.ds(first, piece.shape[0])] = piece[...]
        first += piece.shape[0]
    out[...] = jnp.zeros_like(out)
    count = counts[0, 0]

    def stack_sum(t):
        lefts = [left[lefts_at[g, t]] for g in range(4)]
        rights = [right[rights_at[g, t]] for g in range(4)]
        return jnp.dot(
            jnp.concatenate(lefts, 1),
            jnp.concatenate(rights, 0),
            preferred_element_type=jnp.float32,
        )

    for copy in copies:
        copy.wait()

    def step(i, carry):
        first = i * UNROLL
        sums = [stack_sum(first + u) for u in range(UNROLL)]
        for u in range(UNROLL):
            slot = slots[first + u]
            out[slot] = out[slot] + jnp.where(first + u < count, sums[u], 0.0)
        return carry

    lax.fori_loop(0, lax.div(count + UNROLL - 1, UNROLL), step, 0)


def places_of(lefts, rights):
    za, zb, core, half = (lax.axis_index(a) for a in ("za", "zb", "core", "zh"))
    left = ((lefts & 12) << 2) + ((lefts >> 4) << 2) + ((lefts & 3) ^ (half << 1))
    far = (rights >> 4) ^ za
    near = ((rights >> 2) & 3) ^ zb
    other = ((rights >> 1) & 1) ^ core
    right = (other << 5) + ((far & 1) << 4) + (near << 2) + (far & 2) + (rights & 1)
    return left, right


def body(left_values, right_values, stack_left, stack_right, stack_slot, stack_count):
    own_left = left_values[0]
    own_right = right_values[:, 0]
    right_8 = swap(own_right, "za", Z_HI, 2)
    far_left = swap(own_left, "zh", 2, 1)
    pair = hold(jnp.concatenate([own_right, right_8], 0), "pair", LONG)
    right_4 = swap(pair, "za", Z_HI, 1)
    early = [swap(pair, "zb", Z_LO, k) for k in (1, 2, 3)]
    rest = hold(right_4, "rest", LONG)
    halves = jnp.concatenate([own_left, far_left], 0)
    plane = exchange_plane(jnp.broadcast_to(halves[None], (16,) + halves.shape))
    late = [swap(rest, "zb", Z_LO, k) for k in (1, 2, 3)]
    early = jnp.concatenate([pair] + early, 0)
    late = jnp.concatenate([rest] + late, 0)
    pieces = [early, late]
    pieces += [
        pltpu.with_memory_space_constraint(swap(piece, "core", 2, 1), pltpu.HBM)
        for piece in pieces
    ]
    stack_left, stack_right, late = lax.optimization_barrier((stack_left, stack_right, late))
    lefts_at, rights_at = places_of(stack_left, stack_right)
    block = own_left.shape[1]
    return pl.pallas_call(
        stacks_kernel,
        out_shape=jax.ShapeDtypeStruct((CSLOT, block, block), jnp.float32),
        in_specs=[pl.BlockSpec(memory_space=pltpu.SMEM)] * 4
        + [pl.BlockSpec(memory_space=pltpu.VMEM)] * (1 + len(pieces) // 2)
        + [pl.BlockSpec(memory_space=pltpu.HBM)] * (len(pieces) // 2),
        out_specs=pl.BlockSpec(memory_space=pltpu.VMEM),
        scratch_shapes=[
            pltpu.VMEM((64, block, block), jnp.bfloat16),
            pltpu.SemaphoreType.DMA((len(pieces) // 2,)),
        ],
        compiler_params=pltpu.CompilerParams(vmem_limit_bytes=8 << 20),
    )(
        lefts_at[0, 0].T,
        rights_at[0, 0].T,
        stack_slot[0, 0],
        stack_count,
        plane.reshape(64, block, block),
        *pieces,
    )[None]


def solution(mesh):
    fine = Mesh(mesh.devices.reshape(SIZES), AXES)
    wide, narrow = ("za", "zb", "core"), ("y", "x", "zh")
    return jax.shard_map(
        body,
        mesh=fine,
        in_specs=(
            P(wide, narrow, None, None),
            P(wide, narrow, None, None),
            P(wide, narrow, None, None),
            P(wide, narrow, None, None),
            P(wide, narrow, None),
            P(wide, narrow),
        ),
        out_specs=P(wide, narrow, None, None),
        check_vma=False,
    )
```

```python
import jax
import jax.numpy as jnp
from jax import lax
from jax.experimental import pallas as pl
from jax.experimental.pallas import tpu as pltpu
from jax.sharding import Mesh
from jax.sharding import PartitionSpec as P

CSLOT = 8
UNROLL = 32
Z_HI, Z_LO = 4, 4
AXES = ("za", "zb", "core", "y", "x", "zh")
SIZES = (Z_HI, Z_LO, 2, 4, 4, 2)
LONG = 10**11


def swap(value, axis, size, bits):
    return lax.ppermute(value, axis, [(i, i ^ bits) for i in range(size)])


def exchange_plane(value):
    return lax.all_to_all(value, ("x", "y"), split_axis=0, concat_axis=0, tiled=True)


def hold(value, name, cost=0):
    def kernel(ref, same):
        pass

    return pl.pallas_call(
        kernel,
        out_shape=pltpu.VMEM(value.shape, value.dtype),
        in_specs=[pl.BlockSpec(memory_space=pltpu.VMEM)],
        out_specs=pl.BlockSpec(memory_space=pltpu.VMEM),
        input_output_aliases={0: 0},
        cost_estimate=pl.CostEstimate(flops=cost, bytes_accessed=0, transcendentals=0),
        name=name,
    )(value)


def stacks_kernel(lefts_at, rights_at, slots, counts, left, *refs):
    pieces, (out, right, sems) = refs[:-3], refs[-3:]
    own, other = pieces[: len(pieces) // 2], pieces[len(pieces) // 2 :]
    copies, first = [], 32
    for i, piece in enumerate(other):
        place = right.at[pl.ds(first, piece.shape[0])]
        copies.append(pltpu.make_async_copy(piece, place, sems.at[i]))
        copies[-1].start()
        first += piece.shape[0]
    first = 0
    for piece in own:
        right[pl.ds(first, piece.shape[0])] = piece[...]
        first += piece.shape[0]
    out[...] = jnp.zeros_like(out)
    count = counts[0, 0]

    def stack_sum(t):
        lefts = [left[lefts_at[g, t]] for g in range(4)]
        rights = [right[rights_at[g, t]] for g in range(4)]
        return jnp.dot(
            jnp.concatenate(lefts, 1),
            jnp.concatenate(rights, 0),
            preferred_element_type=jnp.float32,
        )

    for copy in copies:
        copy.wait()

    def step(i, carry):
        first = i * UNROLL
        sums = [stack_sum(first + u) for u in range(UNROLL)]
        for u in range(UNROLL):
            slot = slots[first + u]
            out[slot] = out[slot] + jnp.where(first + u < count, sums[u], 0.0)
        return carry

    lax.fori_loop(0, lax.div(count + UNROLL - 1, UNROLL), step, 0)


def places_of(lefts, rights):
    za, zb, core, half = (lax.axis_index(a) for a in ("za", "zb", "core", "zh"))
    left = ((lefts & 12) << 2) + ((lefts >> 4) << 2) + ((lefts & 3) ^ (half << 1))
    far = (rights >> 4) ^ za
    near = ((rights >> 2) & 3) ^ zb
    other = ((rights >> 1) & 1) ^ core
    right = (other << 5) + ((far & 1) << 4) + (near << 2) + (far & 2) + (rights & 1)
    return left, right


def body(left_values, right_values, stack_left, stack_right, stack_slot, stack_count):
    own_left = left_values[0]
    own_right = right_values[:, 0]
    right_8 = swap(own_right, "za", Z_HI, 2)
    far_left = swap(own_left, "zh", 2, 1)
    pair = hold(jnp.concatenate([own_right, right_8], 0), "pair", LONG)
    right_4 = swap(pair, "za", Z_HI, 1)
    early = [swap(pair, "zb", Z_LO, k) for k in (1, 2, 3)]
    rest = hold(right_4, "rest", LONG)
    halves = jnp.concatenate([own_left, far_left], 0)
    plane = exchange_plane(jnp.broadcast_to(halves[None], (16,) + halves.shape))
    late = [swap(rest, "zb", Z_LO, k) for k in (1, 2, 3)]
    early = jnp.concatenate([pair] + early, 0)
    late = jnp.concatenate([rest] + late, 0)
    pieces = [early, late]
    pieces += [
        pltpu.with_memory_space_constraint(swap(piece, "core", 2, 1), pltpu.HBM)
        for piece in pieces
    ]
    stack_left, stack_right, late = lax.optimization_barrier((stack_left, stack_right, late))
    lefts_at, rights_at = places_of(stack_left, stack_right)
    block = own_left.shape[1]
    return pl.pallas_call(
        stacks_kernel,
        out_shape=jax.ShapeDtypeStruct((CSLOT, block, block), jnp.float32),
        in_specs=[pl.BlockSpec(memory_space=pltpu.SMEM)] * 4
        + [pl.BlockSpec(memory_space=pltpu.VMEM)] * (1 + len(pieces) // 2)
        + [pl.BlockSpec(memory_space=pltpu.HBM)] * (len(pieces) // 2),
        out_specs=pl.BlockSpec(memory_space=pltpu.VMEM),
        scratch_shapes=[
            pltpu.VMEM((64, block, block), jnp.bfloat16),
            pltpu.SemaphoreType.DMA((len(pieces) // 2,)),
        ],
        compiler_params=pltpu.CompilerParams(vmem_limit_bytes=8 << 20),
    )(
        lefts_at[0, 0].T,
        rights_at[0, 0].T,
        stack_slot[0, 0],
        stack_count,
        plane.reshape(64, block, block),
        *pieces,
    )[None]


def solution(mesh):
    fine = Mesh(mesh.devices.reshape(SIZES), AXES)
    wide, narrow = ("za", "zb", "core"), ("y", "x", "zh")
    return jax.shard_map(
        body,
        mesh=fine,
        in_specs=(
            P(wide, narrow, None, None),
            P(wide, narrow, None, None),
            P(wide, narrow, None, None),
            P(wide, narrow, None, None),
            P(wide, narrow, None),
            P(wide, narrow),
        ),
        out_specs=P(wide, narrow, None, None),
        check_vma=False,
    )
```
